256 devices in a mesh: row: 16 (over y, x_hi, core), col: 16 (over z, x_lo).
Axes of the slice: x: 4 (x_hi: 2, x_lo: 2; x = x_hi * 2 + x_lo), y: 4, z: 8, core: 2. Of those that a mesh axis runs over, the one named last changes fastest.
Arguments:
- features: bfloat16 [16, 2048, 256], P('col', 'row'), may hold values from -6 to 6
- weight: bfloat16 [256, 256], replicated, may hold values from -0.375 to 0.375
- cotangent: bfloat16 [32768, 256], P(('row', 'col')), may hold values from -6 to 6
- block_vals: bfloat16 [16, 16, 192, 128, 128], P('row', 'col'), may hold values from -0.0625 to 0.0625
- block_slots: int32 [16, 16, 192], P('row', 'col'), may hold values from 0 to 255, as said below
- block_count: int32 [16, 16], P('row', 'col'), may hold values from 1 to 192, as said below
Outputs:
- activated: bfloat16 [32768, 256], P(('row', 'col'))
- grad_features: float32 [16, 2048, 256], P('col', 'row')
The draws below stay inside these ranges and needn't reach their ends.
Inputs may be any that keep to these rules, and one draw needn't show every extreme that they name: `block_slots`: within one tile the live and the dead slots all name different positions. `block_count`: slots at or past a tile's count are dead and hold arbitrary finite values; some tile is full.
All inputs are finite; a program needn't handle non-finite values.
Results may differ from the reference program's by a relative error of at most 0.0023.
Values may be sent and summed in bfloat16 or wider, within the bound.
A program may use at most 64 MiB of HBM per device.

```python
import math
import jax
import jax.numpy as jnp
from jax import lax

F = 256
BLK = 128
NODE_DEV = 128
NODES = 32768
MAXB = 192
N_ROW = 16
N_COL = 16


def draw_block_slots(key, part):
    key = jax.random.fold_in(key, 11)
    row_blocks = NODE_DEV * N_COL // BLK
    col_blocks = NODE_DEV * N_ROW // BLK
    tile_keys = jax.random.split(key, N_ROW * N_COL)

    def first_slots(tile_key):
        return jax.random.permutation(tile_key, row_blocks * col_blocks)[:MAXB]
    orderings = jax.vmap(first_slots)(tile_keys)
    return orderings.reshape(N_ROW, N_COL, MAXB).astype(jnp.int32)


def draw_block_count(key, part):
    key = jax.random.fold_in(key, 23)
    count_key, pick_key = jax.random.split(key)
    base_draw = jax.random.randint(count_key, (N_ROW * N_COL,), 1, MAXB + 1)
    tile_counts = jnp.maximum(1, base_draw * base_draw // MAXB)
    chosen_tile = jax.random.randint(pick_key, (), 0, N_ROW * N_COL)
    tiles_all = jnp.arange(N_ROW * N_COL, dtype=jnp.int32)
    tile_counts = jnp.where(tiles_all == chosen_tile, MAXB, tile_counts)
    return tile_counts.reshape(N_ROW, N_COL).astype(jnp.int32)


def level_of(key, shape, cuts, smallest, top_value):
    loudness = 1.0
    for axis_at, parts in cuts:
        heights = jax.random.uniform(jax.random.fold_in(jax.random.fold_in(key, 6), axis_at), (parts,), jnp.float32, smallest / len(cuts), top_value / len(cuts))
        loudness = loudness * jnp.repeat(jnp.exp(heights), shape[axis_at] // parts).reshape((-1,) + (1,) * (len(shape) - 1 - axis_at))
    return loudness


def centred(stream_key, dims, spread, reach, shards=(), kind=jnp.bfloat16):
    array = jax.random.normal(stream_key, dims, jnp.float32) * spread
    if len(shards) > 0:
        array = level_of(stream_key, dims, shards, -0.22, 0.18) * array
    return jnp.clip(array, min=-reach, max=reach).astype(kind)


def setup_inputs(seed: int = 0) -> dict:
    arg_keys = jax.random.split(jax.random.key(seed), 7)
    features = centred(arg_keys[0], (N_COL, NODES // N_COL, F), 1.0, 6.0, ((0, 16), (1, 16)))
    weight = centred(arg_keys[1], (F, F), F ** -0.5, 0.375)
    cotangent = centred(arg_keys[2], (NODES, F), 1.0, 6.0, ((0, 256),))
    block_vals = centred(arg_keys[3], (N_ROW, N_COL, MAXB, BLK, BLK), (NODES // 4) ** -0.5, 0.0625, ((0, 16), (1, 16)))
    block_slots = draw_block_slots(jax.random.fold_in(arg_keys[6], 71), 0)
    block_count = draw_block_count(jax.random.fold_in(arg_keys[6], 71), 0)
    return {"features": features, "weight": weight, "cotangent": cotangent, "block_vals": block_vals, "block_slots": block_slots, "block_count": block_count}


exact_precision = lax.Precision.HIGHEST

def gelu_tanh_approx(values):
    return jax.nn.gelu(values, approximate=True)

def tile_apply(values, slot_ids, live_count, source_nodes, dest_blocks, col_blocks, transposed):
    max_slots = values.shape[0]
    block_size = values.shape[1]
    width = source_nodes.shape[-1]
    group_size = math.gcd(max_slots, 32)
    turns = max_slots // group_size
    grouped = values.astype(jnp.float32).reshape(turns, group_size, block_size, block_size)
    slot_groups = slot_ids.reshape(turns, group_size)
    slot_rank = jnp.arange(max_slots, dtype=jnp.int32).reshape(turns, group_size)
    source_span_range = jnp.arange(source_nodes.shape[0], dtype=jnp.int32)
    dest_range = jnp.arange(dest_blocks, dtype=jnp.int32)

    def advance(running, element):
        block_list, position, ranking = element
        if transposed:
            source_idx = position // col_blocks
            dest_idx = position % col_blocks
        else:
            source_idx = position % col_blocks
            dest_idx = position // col_blocks
        selector_function = (source_idx[:, None] == source_span_range[None, :]).astype(jnp.float32)
        selected_entries = jnp.einsum('ld,djk->ljk', selector_function, source_nodes, precision=exact_precision)
        if transposed:
            product = jnp.einsum('gij,gif->gjf', block_list, selected_entries, precision=exact_precision)
        else:
            product = jnp.einsum('gij,gjf->gif', block_list, selected_entries, precision=exact_precision)
        living = (ranking < live_count).astype(jnp.float32)
        position_assigner = (dest_range[:, None] == dest_idx[None, :]).astype(jnp.float32) * living[None, :]
        return (running + jnp.einsum('rg,gif->rif', position_assigner, product, precision=exact_precision), None)
    start = jnp.zeros((dest_blocks, block_size, width), jnp.float32)
    running, _ = lax.scan(advance, start, (grouped, slot_groups, slot_rank))
    return running

def reference(features, weight, cotangent, block_vals, block_slots, block_count):
    block_size = block_vals.shape[-1]
    width = features.shape[-1]
    row_nodes = NODES // N_ROW
    col_nodes = NODES // N_COL
    row_blocks = row_nodes // block_size
    col_blocks = col_nodes // block_size
    panels = features.astype(jnp.float32).reshape(N_COL, col_blocks, block_size, width)

    def row_strip(row_idx):

        def add_tile(running, col_idx):
            term = tile_apply(block_vals[row_idx, col_idx], block_slots[row_idx, col_idx], block_count[row_idx, col_idx], panels[col_idx], row_blocks, col_blocks, False)
            return (running + term, None)
        start = jnp.zeros((row_blocks, block_size, width), jnp.float32)
        running, _ = lax.scan(add_tile, start, jnp.arange(N_COL, dtype=jnp.int32))
        return running
    aggregate = lax.map(row_strip, jnp.arange(N_ROW, dtype=jnp.int32)).reshape(NODES, width)
    weight_wide = weight.astype(jnp.float32)
    mixed_pre = jnp.dot(aggregate, weight_wide, precision=exact_precision)
    activated_full, pullback = jax.vjp(gelu_tanh_approx, mixed_pre)
    activated = activated_full.astype(jnp.bfloat16)
    grad_pre = pullback(cotangent.astype(jnp.float32))[0]
    grad_agg = jnp.dot(grad_pre, weight_wide.T, precision=exact_precision)
    grad_blocks = grad_agg.reshape(N_ROW, row_blocks, block_size, width)

    def col_strip(col_idx):

        def add_tile(running, row_idx):
            term = tile_apply(block_vals[row_idx, col_idx], block_slots[row_idx, col_idx], block_count[row_idx, col_idx], grad_blocks[row_idx], col_blocks, col_blocks, True)
            return (running + term, None)
        start = jnp.zeros((col_blocks, block_size, width), jnp.float32)
        running, _ = lax.scan(add_tile, start, jnp.arange(N_ROW, dtype=jnp.int32))
        return running
    grad_features = lax.map(col_strip, jnp.arange(N_COL, dtype=jnp.int32)).reshape(N_COL, col_nodes, width)
    return (activated, grad_features)
```

```python
import jax
import jax.numpy as jnp
from jax import lax
from jax.experimental import pallas as pl
from jax.experimental.pallas import tpu as pltpu
from jax.sharding import PartitionSpec as P

MESH = pl.DeviceIdType.MESH
BLK = 128
F = 256
SLOTS = 192
NB = 16
NZ = 8
NY = 4
F32 = jnp.float32
BF16 = jnp.bfloat16
LEVELS = 32700.0
N_COPIES = 88
N_LOADS = 4
ROOT = 0.7978845608028654


def power(e):
    return jnp.exp2(e)


def quant(v, dst):
    rows = v.shape[0]
    top = jnp.maximum(jnp.max(jnp.abs(v), axis=0, keepdims=True), 1e-30)
    e = jnp.ceil(jnp.log2(top) + 0.001)
    q = jnp.round(v * (LEVELS * power(-e)))
    dst[0:rows, :] = q.astype(jnp.int32).astype(jnp.int16)
    dst[rows : rows + 16, :] = jnp.broadcast_to(e, (16, v.shape[1])).astype(jnp.int32).astype(jnp.int16)


def dequant(src, rows):
    e = src[rows : rows + 16, :].astype(jnp.int32)[0:1, :].astype(F32)
    return src[0:rows, :].astype(jnp.int32).astype(F32) * (power(e) * (1.0 / LEVELS))


def split3(v):
    hi = v.astype(BF16)
    rest = v - hi.astype(F32)
    mid = rest.astype(BF16)
    lo = (rest - mid.astype(F32)).astype(BF16)
    return jnp.concatenate([hi, mid, lo], axis=0)


def kernel(
    feat, weight, cot, vals_hbm, inv,
    act, gfeat,
    vals, dense, xall, part, gt, qsum,
    h0s, h0r, h0s0, h0r0, h1s, h1r, h1s0, h1r0, xs, xr,
    sibr, ys, yr, ds, dr, tsum,
    send_sem, recv_sem, load_sem,
):
    row = lax.axis_index("row")
    col = lax.axis_index("col")
    core = row % 2
    xh = (row // 2) % 2
    y = row // 4
    z = col // 2
    xl = col % 2
    d = 1 - 2 * core

    def rid(yy, xx, cc):
        return ((yy + 2 * NY) % NY) * 4 + xx * 2 + cc

    def zmod(zz):
        return (zz + 2 * NZ) % NZ

    to_yp = (rid(y + d, xh, core), col)
    to_ym = (rid(y - d, xh, core), col)
    to_xh = (rid(y, 1 - xh, core), col)
    to_sib = (rid(y, xh, 1 - core), col)
    to_zp = (row, zmod(z + 1) * 2 + xl)
    to_zm = (row, zmod(z - 1) * 2 + xl)
    to_xl = (row, z * 2 + 1 - xl)

    copies = []

    def push(src, dst, dev):
        i = len(copies)
        c = pltpu.make_async_remote_copy(
            src_ref=src, dst_ref=dst, send_sem=send_sem.at[i], recv_sem=recv_sem.at[i],
            device_id=dev, device_id_type=MESH,
        )
        c.start()
        copies.append(c)
        return c

    loads = []
    step = SLOTS // N_LOADS
    for i in range(N_LOADS):
        c = pltpu.make_async_copy(vals_hbm.at[pl.ds(i * step, step)], vals.at[pl.ds(i * step, step)], load_sem.at[i])
        c.start()
        loads.append(c)

    barrier = pltpu.get_barrier_semaphore()
    for dev in (to_yp, to_ym, to_xh, to_sib, to_zp, to_zm, to_xl):
        pl.semaphore_signal(barrier, inc=1, device_id=dev, device_id_type=MESH)

    def xat(r):
        return xall.at[pl.ds(pl.multiple_of(r * BLK, BLK), BLK)]

    xat(row)[...] = feat[0]
    vals[SLOTS] = jnp.zeros((BLK, BLK), BF16)
    pl.semaphore_wait(barrier, 7)

    def put(r, dev):
        return push(xat(r), xat(r), dev)

    r_x = rid(y, 1 - xh, core)
    r_m = rid(y - d, xh, core)
    r_p = rid(y + d, xh, core)
    r_mx = rid(y - d, 1 - xh, core)
    r_px = rid(y + d, 1 - xh, core)
    r_o = rid(y + 2, xh, core)
    r_ox = rid(y + 2, 1 - xh, core)
    a_x = put(row, to_xh)
    a_p = put(row, to_yp)
    a_m = put(row, to_ym)
    sib = [put(row, to_sib)]

    def build(lo, hi):
        def one(r, carry):
            for c in range(NB):
                dense[pl.ds(pl.multiple_of(r * BLK, BLK), BLK), c * BLK : (c + 1) * BLK] = vals[inv[r * NB + c]]
            return carry

        lax.fori_loop(lo, hi, one, 0)

    a_p.wait_recv()
    a_o = put(r_m, to_yp)
    a_x.wait_recv()
    a_px = put(r_x, to_yp)
    a_mx = put(r_x, to_ym)
    sib.append(put(r_m, to_sib))
    sib.append(put(r_x, to_sib))
    a_m.wait_recv()
    sib.append(put(r_p, to_sib))
    for c in loads:
        c.wait()
    build(0, 6)
    a_px.wait_recv()
    a_ox = put(r_mx, to_yp)
    a_o.wait_recv()
    sib.append(put(r_mx, to_sib))
    sib.append(put(r_o, to_sib))
    build(6, 11)
    a_mx.wait_recv()
    sib.append(put(r_px, to_sib))
    build(11, 16)
    a_ox.wait_recv()
    sib.append(put(r_ox, to_sib))
    for c in sib:
        c.wait_recv()

    targets = [z + 4, z + 3, z - 3, z + 2, z - 2, z + 1, z - 1, z]
    own_rows = pl.ds(pl.multiple_of(xl * BLK, BLK), BLK)
    far_rows = pl.ds(pl.multiple_of((1 - xl) * BLK, BLK), BLK)
    x_copy = {}

    def forward(i):
        t = zmod(targets[i])
        part[i] = jnp.dot(
            dense[pl.ds(pl.multiple_of(t * 2 * BLK, 2 * BLK), 2 * BLK), :], xall[...], preferred_element_type=F32
        )
        quant(part[i, far_rows, BLK:F], xs.at[i])
        x_copy[i] = push(xs.at[i], xr.at[i], to_xl)

    forward(0)
    quant(part[0, 0:BLK, 0:BLK], h0s0.at[0])
    h0p = push(h0s0.at[0], h0r0.at[0], to_zp)
    quant(part[0, BLK : 2 * BLK, 0:BLK], h0s0.at[1])
    h0m = push(h0s0.at[1], h0r0.at[1], to_zm)
    forward(1)
    forward(2)

    def mine(i):
        x_copy[i].wait_recv()
        return part[i, own_rows, BLK:F] + dequant(xr.at[i], BLK)

    first = mine(0)
    quant(first[0:64], h1s0.at[0])
    h1p = push(h1s0.at[0], h1r0.at[0], to_zp)
    quant(first[64:128], h1s0.at[1])
    h1m = push(h1s0.at[1], h1r0.at[1], to_zm)

    def chain0(s, way, i, copy, dev):
        copy.wait_recv()
        out = h0s.at[way, s]
        if s == 0:
            got = dequant(h0r0.at[way], BLK)
            kept = part[i, :, 0:BLK]
            if way == 0:
                v = jnp.concatenate([kept[0:BLK] + got, kept[BLK : 2 * BLK]], axis=0)
            else:
                v = jnp.concatenate([kept[0:BLK], kept[BLK : 2 * BLK] + got], axis=0)
        else:
            v = part[i, :, 0:BLK] + dequant(h0r.at[way, s - 1], 2 * BLK)
        quant(v, out)
        return push(out, h0r.at[way, s], dev)

    def chain1(s, way, i, copy, dev):
        kept = mine(i)
        copy.wait_recv()
        out = h1s.at[way, s]
        if s == 0:
            got = dequant(h1r0.at[way], 64)
            if way == 0:
                v = jnp.concatenate([kept[0:64] + got, kept[64:128]], axis=0)
            else:
                v = jnp.concatenate([kept[0:64], kept[64:128] + got], axis=0)
        else:
            v = kept + dequant(h1r.at[way, s - 1], BLK)
        quant(v, out)
        return push(out, h1r.at[way, s], dev)

    for s in range(3):
        h0p = chain0(s, 0, 1 + 2 * s, h0p, to_zp)
        h0m = chain0(s, 1, 2 + 2 * s, h0m, to_zm)
        if s < 2:
            forward(3 + 2 * s)
            forward(4 + 2 * s)
        else:
            forward(7)
        h1p = chain1(s, 0, 1 + 2 * s, h1p, to_zp)
        h1m = chain1(s, 1, 2 + 2 * s, h1m, to_zm)

    h0p.wait_recv()
    h0m.wait_recv()
    part[7, :, 0:BLK] = part[7, :, 0:BLK] + dequant(h0r.at[0, 2], 2 * BLK) + dequant(h0r.at[1, 2], 2 * BLK)
    quant(part[7, far_rows, 0:BLK], xs.at[8])
    x_last = push(xs.at[8], xr.at[8], to_xl)
    right = mine(7)
    h1p.wait_recv()
    h1m.wait_recv()
    right = right + dequant(h1r.at[0, 2], BLK) + dequant(h1r.at[1, 2], BLK)
    x_last.wait_recv()
    left = part[7, own_rows, 0:BLK] + dequant(xr.at[8], BLK)
    agg = jnp.concatenate([left, right], axis=1)

    w = weight[...]
    three = jnp.dot(split3(agg), w, preferred_element_type=F32)
    v = three[0:BLK] + three[BLK : 2 * BLK] + three[2 * BLK : 3 * BLK]
    v2 = v * v
    th = jnp.tanh(ROOT * (v + 0.044715 * (v2 * v)))
    act[...] = (0.5 * v * (1.0 + th)).astype(BF16)
    slope = 0.5 * (1.0 + th) + (0.5 * ROOT) * v * (1.0 - th * th) * (1.0 + 3 * 0.044715 * v2)
    grad_pre = cot[...].astype(F32) * slope
    tri = lax.dot_general(w, split3(grad_pre), (((1,), (1,)), ((), ())), preferred_element_type=F32)
    gt[col] = (tri[:, 0:BLK] + tri[:, BLK : 2 * BLK] + tri[:, 2 * BLK : 3 * BLK]).astype(BF16)

    def spot(zz, lane, lo, hi):
        return gt.at[zmod(zz) * 2 + lane, lo:hi]

    def send(zz, lane, lo, hi, dev):
        return push(spot(zz, lane, lo, hi), spot(zz, lane, lo, hi), dev)

    far = 1 - xl
    x0 = send(z, xl, 0, BLK, to_xl)
    op = send(z, xl, 0, F, to_zp)
    om = send(z, xl, 0, F, to_zm)
    xf = {0: [send(z, xl, BLK, F, to_xl)]}
    x0.wait_recv()
    pp = send(z, far, 0, BLK, to_zp)
    pm = send(z, far, 0, BLK, to_zm)

    def product(zz, n):
        t = zmod(zz)
        lhs = jnp.concatenate([gt[t * 2], gt[t * 2 + 1]], axis=1)
        rhs = dense[pl.ds(pl.multiple_of(t * 2 * BLK, 2 * BLK), 2 * BLK), pl.ds(pl.multiple_of(n * 2 * BLK, 2 * BLK), 2 * BLK)]
        return jnp.dot(lhs, rhs, preferred_element_type=F32)

    def add_pass(zs, fresh):
        def one(n, carry):
            total = product(zs[0], n)
            for zz in zs[1:]:
                total = total + product(zz, n)
            if fresh:
                qsum[2 * n] = total[:, 0:BLK]
                qsum[2 * n + 1] = total[:, BLK:F]
            else:
                qsum[2 * n] = qsum[2 * n] + total[:, 0:BLK]
                qsum[2 * n + 1] = qsum[2 * n + 1] + total[:, BLK:F]
            return carry

        lax.fori_loop(0, NB // 2, one, 0)

    for s in range(1, 4):
        op.wait_recv()
        om.wait_recv()
        if s < 3:
            op = send(z - s, xl, 0, F, to_zp)
            om = send(z + s, xl, 0, F, to_zm)
        else:
            op = send(z - s, xl, 0, BLK, to_zp)
            om = send(z + s, xl, BLK, F, to_zm)
        xf[s] = [send(z - s, xl, BLK, F, to_xl), send(z + s, xl, BLK, F, to_xl)]
        pp.wait_recv()
        pm.wait_recv()
        if s < 3:
            pp = send(z - s, far, 0, BLK, to_zp)
            pm = send(z + s, far, 0, BLK, to_zm)
        else:
            pp = send(z - s, far, 0, 64, to_zp)
            pm = send(z + s, far, 64, BLK, to_zm)
        for c in xf[s - 1]:
            c.wait_recv()
        add_pass([z] if s == 1 else [z - s + 1, z + s - 1], s == 1)
    om.wait_recv()
    op.wait_recv()
    xf[4] = [send(z + 4, xl, BLK, F, to_xl)]
    for c in xf[3]:
        c.wait_recv()
    add_pass([z - 3, z + 3], False)
    pp.wait_recv()
    pm.wait_recv()
    xf[4][0].wait_recv()

    order = [(y + 2, 0), (y + 2, 1), (y + 1, 0), (y + 1, 1), (y - 1, 0), (y - 1, 1), (y, 0), (y, 1)]
    from_sib = []
    for i, (yy, xx) in enumerate(order):
        n = ((yy + 2 * NY) % NY) * 2 + xx
        total = product(z + 4, n)
        qsum[2 * n] = qsum[2 * n] + total[:, 0:BLK]
        qsum[2 * n + 1] = qsum[2 * n + 1] + total[:, BLK:F]
        from_sib.append(push(qsum.at[2 * n + 1 - core], sibr.at[n], to_sib))

    def pair(yy, xx):
        n = ((yy + 2 * NY) % NY) * 2 + xx
        return qsum[2 * n + core] + sibr[n]

    for c in from_sib[0:2]:
        c.wait_recv()
    for k in range(2):
        quant(pair(y + 2, k), ys.at[0, k])
    y1 = push(ys.at[0], yr.at[0], to_yp)
    for c in from_sib[2:6]:
        c.wait_recv()
    for k in range(2):
        quant(pair(y - d, k), ys.at[1, k])
    y2 = push(ys.at[1], yr.at[1], to_ym)
    for k in range(2):
        tsum[k] = pair(y + d, k)
    y1.wait_recv()
    for k in range(2):
        quant(tsum[k] + dequant(yr.at[0, k], F), ys.at[2, k])
    y3 = push(ys.at[2], yr.at[2], to_yp)
    for c in from_sib[6:8]:
        c.wait_recv()
    for k in range(2):
        tsum[k] = pair(y, k)
    y2.wait_recv()
    y3.wait_recv()
    for k in range(2):
        tsum[k] = tsum[k] + dequant(yr.at[1, k], F) + dequant(yr.at[2, k], F)
    quant(tsum[1 - xh], ds)
    last = push(ds, dr, to_xh)
    last.wait_recv()
    gfeat[0] = (tsum[xh] + dequant(dr, F)).T

    for c in copies:
        c.wait_send()


def body(features, weight, cotangent, block_vals, block_slots, block_count):
    slots = block_slots[0, 0]
    ids = lax.broadcasted_iota(jnp.int32, (SLOTS, NB * NB), 0)
    place = lax.broadcasted_iota(jnp.int32, (SLOTS, NB * NB), 1)
    hit = (slots[:, None] == place) & (ids < block_count[0, 0])
    inv = SLOTS - jnp.sum(jnp.where(hit, SLOTS - ids, 0), axis=0, dtype=jnp.int32)
    vm = pl.BlockSpec(memory_space=pltpu.VMEM)
    i16 = jnp.int16
    v = pltpu.VMEM
    return pl.pallas_call(
        kernel,
        out_shape=(
            jax.ShapeDtypeStruct((BLK, F), BF16),
            jax.ShapeDtypeStruct((1, BLK, F), F32),
        ),
        in_specs=[vm, vm, vm, pl.BlockSpec(memory_space=pl.ANY), pl.BlockSpec(memory_space=pltpu.SMEM)],
        out_specs=(vm, vm),
        scratch_shapes=[
            v((SLOTS + 1, BLK, BLK), BF16),
            v((NB * BLK, NB * BLK), BF16),
            v((NB * BLK, F), BF16),
            v((8, 2 * BLK, F), F32),
            v((NB, F, BLK), BF16),
            v((NB, F, BLK), F32),
            v((2, 3, 2 * BLK + 16, BLK), i16),
            v((2, 3, 2 * BLK + 16, BLK), i16),
            v((2, BLK + 16, BLK), i16),
            v((2, BLK + 16, BLK), i16),
            v((2, 3, BLK + 16, BLK), i16),
            v((2, 3, BLK + 16, BLK), i16),
            v((2, 80, BLK), i16),
            v((2, 80, BLK), i16),
            v((9, BLK + 16, BLK), i16),
            v((9, BLK + 16, BLK), i16),
            v((8, F, BLK), F32),
            v((3, 2, F + 16, BLK), i16),
            v((3, 2, F + 16, BLK), i16),
            v((F + 16, BLK), i16),
            v((F + 16, BLK), i16),
            v((2, F, BLK), F32),
            pltpu.SemaphoreType.DMA((N_COPIES,)),
            pltpu.SemaphoreType.DMA((N_COPIES,)),
            pltpu.SemaphoreType.DMA((N_LOADS,)),
        ],
        compiler_params=pltpu.CompilerParams(
            collective_id=0, has_side_effects=True, vmem_limit_bytes=48 * 1024 * 1024
        ),
        name="layer",
    )(features, weight, cotangent, block_vals.reshape(SLOTS, BLK, BLK), inv)


def solution(mesh):
    return jax.shard_map(
        body,
        mesh=mesh,
        in_specs=(
            P("col", "row", None),
            P(),
            P(("row", "col"), None),
            P("row", "col", None, None, None),
            P("row", "col", None),
            P("row", "col"),
        ),
        out_specs=(P(("row", "col"), None), P("col", "row", None)),
        check_vma=False,
    )
```

```python
import jax
import jax.numpy as jnp
from jax import lax
from jax.experimental import pallas as pl
from jax.experimental.pallas import tpu as pltpu
from jax.sharding import PartitionSpec as P

MESH = pl.DeviceIdType.MESH
BLK = 128
F = 256
SLOTS = 192
NB = 16
NZ = 8
NY = 4
F32 = jnp.float32
BF16 = jnp.bfloat16
LEVELS = 32700.0
N_COPIES = 96
N_LOADS = 4
ROOT = 0.7978845608028654


def quant(v, dst):
    rows = v.shape[0]
    top = jnp.maximum(jnp.max(jnp.abs(v), axis=0, keepdims=True), 1e-30)
    e = jnp.ceil(jnp.log2(top) + 0.001)
    q = jnp.round(v * (LEVELS * jnp.exp2(-e)))
    dst[0:rows, :] = q.astype(jnp.int32).astype(jnp.int16)
    dst[rows : rows + 16, :] = jnp.broadcast_to(e, (16, v.shape[1])).astype(jnp.int32).astype(jnp.int16)


def dequant(src):
    rows = src.shape[0] - 16
    e = src[rows : rows + 16, :].astype(jnp.int32)[0:1, :].astype(F32)
    return src[0:rows, :].astype(jnp.int32).astype(F32) * (jnp.exp2(e) * (1.0 / LEVELS))


def split3(v):
    hi = v.astype(BF16)
    rest = v - hi.astype(F32)
    mid = rest.astype(BF16)
    lo = (rest - mid.astype(F32)).astype(BF16)
    return jnp.concatenate([hi, mid, lo], axis=0)


def kernel(
    feat_hbm, weight_hbm, cot_hbm, vals_hbm, slots_hbm, count,
    act, gfeat,
    weight, cot, slots, inv_v, inv, vals, dense, xall, part, gt, qsum,
    xs, xr, ns, nr, fs, fr, ms, mr, es, er, sibr, ds, dr,
    send_sem, recv_sem, load_sem,
):
    row = lax.axis_index("row")
    col = lax.axis_index("col")
    core = row % 2
    xh = (row // 2) % 2
    y = row // 4
    z = col // 2
    xl = col % 2

    def rid(yy, xx, cc):
        return ((yy + 2 * NY) % NY) * 4 + xx * 2 + cc

    def zmod(zz):
        return (zz + 2 * NZ) % NZ

    def swap(b, k):
        return 1 - b if k else b

    row_moves = [(2, 1), (1, 1), (-1, 1), (2, 0), (0, 1), (1, 0), (-1, 0)]
    row_devs = [(rid(y + dy, swap(xh, dx), core), col) for dy, dx in row_moves]
    z_devs = [(row, zmod(z + dz) * 2 + xl) for dz in (2, -2, 1, -1)]
    to_sib = (rid(y, xh, 1 - core), col)
    to_xl = (row, z * 2 + 1 - xl)

    copies = []

    def push(src, dst, dev):
        i = len(copies)
        c = pltpu.make_async_remote_copy(
            src_ref=src, dst_ref=dst, send_sem=send_sem.at[i], recv_sem=recv_sem.at[i],
            device_id=dev, device_id_type=MESH,
        )
        c.start()
        copies.append(c)
        return c

    barrier = pltpu.get_barrier_semaphore()
    for dev in row_devs + z_devs + [to_sib, to_xl]:
        pl.semaphore_signal(barrier, inc=1, device_id=dev, device_id_type=MESH)

    def xat(r):
        return xall.at[pl.ds(pl.multiple_of(r * BLK, BLK), BLK)]

    loads = []

    def load(src, dst):
        c = pltpu.make_async_copy(src, dst, load_sem.at[len(loads)])
        c.start()
        loads.append(c)

    load(feat_hbm.at[0], xat(row))
    load(slots_hbm.at[0], slots)
    step = SLOTS // N_LOADS
    for i in range(N_LOADS):
        load(vals_hbm.at[pl.ds(i * step, step)], vals.at[pl.ds(i * step, step)])
    load(weight_hbm, weight)
    load(cot_hbm, cot)
    vals[SLOTS] = jnp.zeros((BLK, BLK), BF16)
    loads[1].wait()
    place = lax.broadcasted_iota(jnp.int32, (NB * NB, SLOTS), 0)
    ids = lax.broadcasted_iota(jnp.int32, (NB * NB, SLOTS), 1)
    hit = jnp.where((slots[...] == place) & (ids < count[0, 0]), 1.0, 0.0).astype(BF16)
    marks = (SLOTS - lax.broadcasted_iota(jnp.int32, (8, SLOTS), 1)).astype(F32).astype(BF16)
    found = lax.dot_general(marks, hit, (((1,), (1,)), ((), ())), preferred_element_type=F32)
    inv_v[...] = SLOTS - found.astype(jnp.int32)
    to_smem = pltpu.make_async_copy(inv_v, inv, load_sem.at[len(loads)])
    to_smem.start()
    loads[0].wait()
    pl.semaphore_wait(barrier, len(row_devs) + len(z_devs) + 2)

    def put(r, dev):
        return push(xat(r), xat(r), dev)

    feats = [put(row, dev) for dev in row_devs]
    sib = [put(row, to_sib)]

    def build(lo, hi):
        def one(r, carry):
            for c in range(NB):
                dense[pl.ds(pl.multiple_of(r * BLK, BLK), BLK), c * BLK : (c + 1) * BLK] = vals[jnp.clip(inv[0, r * NB + c], 0, SLOTS)]
            return carry

        lax.fori_loop(lo, hi, one, 0)

    to_smem.wait()
    for c in loads[2:]:
        c.wait()
    build(0, NB)
    for i in (5, 6, 4, 3, 1, 2, 0):
        dy, dx = row_moves[i]
        feats[i].wait_recv()
        sib.append(put(rid(y - dy, swap(xh, dx), core), to_sib))
    for c in sib:
        c.wait_recv()

    own_rows = pl.ds(pl.multiple_of(xl * BLK, BLK), BLK)
    far_rows = pl.ds(pl.multiple_of((1 - xl) * BLK, BLK), BLK)
    moves = [4, 3, -3, 1, -1, 2, -2, 0]
    to_z = {k: (row, zmod(z + k) * 2 + xl) for k in (1, -1, 2, -2)}
    half = [slice(0, BLK), slice(BLK, F)]
    x_copy = {}
    near = {}

    def forward(i):
        t = zmod(z + moves[i])
        part[i] = jnp.dot(
            dense[pl.ds(pl.multiple_of(t * 2 * BLK, 2 * BLK), 2 * BLK), :], xall[...], preferred_element_type=F32
        )

    def cross(i, h):
        quant(part[i, far_rows, half[h]], xs.at[h, i])
        x_copy[i, h] = push(xs.at[h, i], xr.at[h, i], to_xl)

    def joined(i, h):
        x_copy[i, h].wait_recv()
        return part[i, own_rows, half[h]] + dequant(xr.at[h, i])

    def pass_on(v, src, dst, dev):
        quant(v, src)
        return push(src, dst, dev)

    for i in range(8):
        forward(i)
        if i in (3, 4):
            for h in range(2):
                near[i - 3, h] = pass_on(part[i, :, half[h]], ns.at[h, i - 3], nr.at[h, i - 3], to_z[moves[i]])
        elif i < 7:
            cross(i, 0)
        if i == 5:
            cross(0, 1)
            cross(1, 1)
    for i in (2, 5, 6):
        cross(i, 1)
    four = {}
    three = {}
    for h in range(2):
        four[h] = pass_on(joined(0, h), fs.at[h], fr.at[h], to_z[2 - 4 * h])
        for k in range(2):
            three[k, h] = pass_on(joined(1 + k, h), ms.at[h, k], mr.at[h, k], to_z[1 - 2 * k])
        if h == 0:
            for k in range(4):
                near[k % 2, k // 2].wait_recv()
            for q in range(2):
                part[7, :, half[q]] = part[7, :, half[q]] + dequant(nr.at[q, 0]) + dequant(nr.at[q, 1])
                cross(7, q)
    last = {}
    for h in range(2):
        for k in range(2):
            v = joined(5 + k, h)
            three[k, h].wait_recv()
            v = v + dequant(mr.at[h, k])
            if h == k:
                four[h].wait_recv()
                v = v + dequant(fr.at[h])
            last[k, h] = pass_on(v, es.at[h, k], er.at[h, k], to_z[2 - 4 * k])
    total = []
    for h in range(2):
        v = joined(7, h)
        for k in range(2):
            last[k, h].wait_recv()
            v = v + dequant(er.at[h, k])
        total.append(v)
    agg = jnp.concatenate(total, axis=1)

    w = weight[...]
    three = jnp.dot(split3(agg), w, preferred_element_type=F32)
    v = three[0:BLK] + three[BLK : 2 * BLK] + three[2 * BLK : 3 * BLK]
    v2 = v * v
    th = jnp.tanh(ROOT * (v + 0.044715 * (v2 * v)))
    act[...] = (0.5 * v * (1.0 + th)).astype(BF16)
    slope = 0.5 * (1.0 + th) + (0.5 * ROOT) * v * (1.0 - th * th) * (1.0 + 3 * 0.044715 * v2)
    grad_pre = cot[...].astype(F32) * slope
    tri = lax.dot_general(w, split3(grad_pre), (((1,), (1,)), ((), ())), preferred_element_type=F32)
    gt[col] = (tri[:, 0:BLK] + tri[:, BLK : 2 * BLK] + tri[:, 2 * BLK : 3 * BLK]).astype(BF16)

    far = 1 - xl

    def send(zz, lane, h, dev):
        spot = gt.at[zmod(zz) * 2 + lane, half[h]]
        return push(spot, spot, dev)

    g = {}
    for h in range(2):
        for k in (2, -2):
            g[k, h] = send(z, xl, h, to_z[k])
        g[0, h] = send(z, xl, h, to_xl)
        for k in (1, -1):
            g[k, h] = send(z, xl, h, to_z[k])

    def product(zz, n):
        t = zmod(zz)
        lhs = jnp.concatenate([gt[t * 2], gt[t * 2 + 1]], axis=1)
        rhs = dense[pl.ds(pl.multiple_of(t * 2 * BLK, 2 * BLK), 2 * BLK), pl.ds(pl.multiple_of(n * 2 * BLK, 2 * BLK), 2 * BLK)]
        return jnp.dot(lhs, rhs, preferred_element_type=F32)

    def add_to(zs_, n, fresh):
        total = product(zs_[0], n)
        for zz in zs_[1:]:
            total = total + product(zz, n)
        if fresh:
            qsum[2 * n] = total[:, 0:BLK]
            qsum[2 * n + 1] = total[:, BLK:F]
        else:
            qsum[2 * n] = qsum[2 * n] + total[:, 0:BLK]
            qsum[2 * n + 1] = qsum[2 * n + 1] + total[:, BLK:F]

    def add_pass(zs_, fresh):
        for n in range(NB // 2):
            add_to(zs_, n, fresh)

    relay = {}
    beside = {}
    onto = {}
    for h in range(2):
        for k in (2, -2):
            one = k // 2
            g[k, h].wait_recv()
            relay[3 * one, h] = send(z - k, xl, h, to_z[one])
            if h == (1 - one) // 2:
                relay[4, h] = send(z - k, xl, h, to_z[k])
            onto[k, h] = send(z - k, xl, h, to_xl)
        g[0, h].wait_recv()
        for k in (1, -1):
            beside[k, h] = send(z, far, h, to_z[k])
    add_pass([z], True)
    for h in range(2):
        for k in (3, -3, 4):
            relay[k, h].wait_recv()
            onto[k, h] = send(z - k, xl, h, to_xl)
    for h in range(2):
        for k in (1, -1):
            g[k, h].wait_recv()
            beside[k, h].wait_recv()
        for k in (2, -2):
            onto[k, h].wait_recv()
    add_pass([z - 1, z + 1, z - 2, z + 2], False)
    for h in range(2):
        for k in (3, -3, 4):
            onto[k, h].wait_recv()

    order = row_moves + [(0, 0)]
    from_sib = []
    sums = []

    def settle(i):
        dy, dx = order[i]
        n = rid(y + dy, swap(xh, dx), 0) // 2
        from_sib[i].wait_recv()
        value = qsum[2 * n + core] + sibr[i]
        if i < 7:
            quant(value, ds.at[i])
            sums.append(push(ds.at[i], dr.at[i], row_devs[i]))
        return value

    for i, (dy, dx) in enumerate(order):
        n = rid(y + dy, swap(xh, dx), 0) // 2
        add_to([z + 3, z - 3, z + 4], n, False)
        from_sib.append(push(qsum.at[2 * n + 1 - core], sibr.at[i], to_sib))
        if i >= 2:
            settle(i - 2)
    settle(6)
    total = settle(7)
    for i in (5, 6, 4, 3, 1, 2, 0):
        sums[i].wait_recv()
        total = total + dequant(dr.at[i])
    gfeat[0] = total.T

    for c in copies:
        c.wait_send()


def body(features, weight, cotangent, block_vals, block_slots, block_count):
    vm = pl.BlockSpec(memory_space=pltpu.VMEM)
    hbm = pl.BlockSpec(memory_space=pl.ANY)
    v = pltpu.VMEM
    coded = (F + 16, BLK)
    small = (BLK + 16, BLK)
    i16 = jnp.int16
    return pl.pallas_call(
        kernel,
        out_shape=(
            jax.ShapeDtypeStruct((BLK, F), BF16),
            jax.ShapeDtypeStruct((1, BLK, F), F32),
        ),
        in_specs=[hbm] * 5 + [pl.BlockSpec(memory_space=pltpu.SMEM)],
        out_specs=(vm, vm),
        scratch_shapes=[
            v((F, F), BF16),
            v((BLK, F), BF16),
            v((1, SLOTS), jnp.int32),
            v((8, NB * NB), jnp.int32),
            pltpu.SMEM((8, NB * NB), jnp.int32),
            v((SLOTS + 1, BLK, BLK), BF16),
            v((NB * BLK, NB * BLK), BF16),
            v((NB * BLK, F), BF16),
            v((8, 2 * BLK, F), F32),
            v((NB, F, BLK), BF16),
            v((NB, F, BLK), F32),
            v((2, 8, *small), i16),
            v((2, 8, *small), i16),
            v((2, 2, *coded), i16),
            v((2, 2, *coded), i16),
            v((2, *small), i16),
            v((2, *small), i16),
            v((2, 2, *small), i16),
            v((2, 2, *small), i16),
            v((2, 2, *small), i16),
            v((2, 2, *small), i16),
            v((8, F, BLK), F32),
            v((7, *coded), i16),
            v((7, *coded), i16),
            pltpu.SemaphoreType.DMA((N_COPIES,)),
            pltpu.SemaphoreType.DMA((N_COPIES,)),
            pltpu.SemaphoreType.DMA((N_LOADS + 6,)),
        ],
        compiler_params=pltpu.CompilerParams(
            collective_id=0, has_side_effects=True, vmem_limit_bytes=56 * 1024 * 1024
        ),
        name="layer",
    )(features, weight, cotangent, block_vals.reshape(SLOTS, BLK, BLK), block_slots, block_count)


def solution(mesh):
    return jax.shard_map(
        body,
        mesh=mesh,
        in_specs=(
            P("col", "row", None),
            P(),
            P(("row", "col"), None),
            P("row", "col", None, None, None),
            P("row", "col", None),
            P("row", "col"),
        ),
        out_specs=(P(("row", "col"), None), P("col", "row", None)),
        check_vma=False,
    )
```

```python
import jax
import jax.numpy as jnp
from jax import lax
from jax.experimental import pallas as pl
from jax.experimental.pallas import tpu as pltpu
from jax.sharding import PartitionSpec as P

MESH = pl.DeviceIdType.MESH
BLK = 128
F = 256
SLOTS = 192
NB = 16
NZ = 8
NY = 4
F32 = jnp.float32
BF16 = jnp.bfloat16
LEVELS = 32700.0
N_COPIES = 128
N_LOADS = 4
ROOT = 0.7978845608028654


def quant(v, dst):
    rows = v.shape[0]
    top = jnp.maximum(jnp.max(jnp.abs(v), axis=0, keepdims=True), 1e-30)
    e = jnp.ceil(jnp.log2(top) + 0.001)
    q = jnp.round(v * (LEVELS * jnp.exp2(-e)))
    dst[0:rows, :] = q.astype(jnp.int32).astype(jnp.int16)
    dst[rows : rows + 16, :] = jnp.broadcast_to(e, (16, v.shape[1])).astype(jnp.int32).astype(jnp.int16)


def dequant(src):
    rows = src.shape[0] - 16
    e = src[rows : rows + 16, :].astype(jnp.int32)[0:1, :].astype(F32)
    return src[0:rows, :].astype(jnp.int32).astype(F32) * (jnp.exp2(e) * (1.0 / LEVELS))


def split3(v):
    hi = v.astype(BF16)
    rest = v - hi.astype(F32)
    mid = rest.astype(BF16)
    lo = (rest - mid.astype(F32)).astype(BF16)
    return jnp.concatenate([hi, mid, lo], axis=0)


def kernel(
    feat_hbm, weight_hbm, cot_hbm, vals_hbm, slots_hbm, count_hbm,
    act, gfeat,
    weight, cot, slots, count, inv_v, inv, vals, dense, xall, part, gt, qsum,
    xs, xr, ns, nr, fs, fr, ms, mr, es, er, sibr, ds, dr,
    send_sem, recv_sem, load_sem,
):
    row = lax.axis_index("row")
    col = lax.axis_index("col")
    core = row % 2
    xh = (row // 2) % 2
    y = row // 4
    z = col // 2
    xl = col % 2

    def rid(yy, xx, cc):
        return ((yy + 2 * NY) % NY) * 4 + xx * 2 + cc

    def zmod(zz):
        return (zz + 2 * NZ) % NZ

    def swap(b, k):
        return 1 - b if k else b

    row_moves = [(2, 1), (1, 1), (-1, 1), (2, 0), (0, 1), (1, 0), (-1, 0)]
    row_devs = [(rid(y + dy, swap(xh, dx), core), col) for dy, dx in row_moves]
    z_devs = [(row, zmod(z + dz) * 2 + xl) for dz in (2, -2, 1, -1)]
    to_sib = (rid(y, xh, 1 - core), col)
    to_xl = (row, z * 2 + 1 - xl)

    copies = []

    def push(src, dst, dev):
        i = len(copies)
        c = pltpu.make_async_remote_copy(
            src_ref=src, dst_ref=dst, send_sem=send_sem.at[i], recv_sem=recv_sem.at[i],
            device_id=dev, device_id_type=MESH,
        )
        c.start()
        copies.append(c)
        return c

    barrier = pltpu.get_barrier_semaphore()
    for dev in row_devs + z_devs + [to_sib, to_xl]:
        pl.semaphore_signal(barrier, inc=1, device_id=dev, device_id_type=MESH)

    half = [slice(0, BLK), slice(BLK, F)]

    def xat(h, r):
        return xall.at[h, pl.ds(pl.multiple_of(r * BLK, BLK), BLK)]

    loads = []

    def load(src, dst):
        c = pltpu.make_async_copy(src, dst, load_sem.at[len(loads)])
        c.start()
        loads.append(c)

    for h in range(2):
        load(feat_hbm.at[0, :, half[h]], xat(h, row))
    load(slots_hbm.at[0], slots)
    load(count_hbm, count)
    step = SLOTS // N_LOADS
    for i in range(N_LOADS):
        load(vals_hbm.at[pl.ds(i * step, step)], vals.at[pl.ds(i * step, step)])
    load(weight_hbm, weight)
    load(cot_hbm, cot)
    vals[SLOTS] = jnp.zeros((BLK, BLK), BF16)
    loads[2].wait()
    loads[3].wait()
    place = lax.broadcasted_iota(jnp.int32, (NB * NB, SLOTS), 0)
    ids = lax.broadcasted_iota(jnp.int32, (NB * NB, SLOTS), 1)
    hit = jnp.where((slots[...] == place) & (ids < count[...]), 1.0, 0.0).astype(BF16)
    marks = (SLOTS - lax.broadcasted_iota(jnp.int32, (8, SLOTS), 1)).astype(F32).astype(BF16)
    found = lax.dot_general(marks, hit, (((1,), (1,)), ((), ())), preferred_element_type=F32)
    inv_v[...] = SLOTS - found.astype(jnp.int32)
    to_smem = pltpu.make_async_copy(inv_v, inv, load_sem.at[len(loads)])
    to_smem.start()
    loads[0].wait()
    loads[1].wait()
    pl.semaphore_wait(barrier, len(row_devs) + len(z_devs) + 2)

    def put(h, r, dev):
        return push(xat(h, r), xat(h, r), dev)

    feats = []
    sib = []
    for h in range(2):
        feats.append([put(h, row, dev) for dev in row_devs])
        sib.append([put(h, row, to_sib)])

    def build(lo, hi):
        def one(r, carry):
            for c in range(NB):
                dense[pl.ds(pl.multiple_of(r * BLK, BLK), BLK), c * BLK : (c + 1) * BLK] = vals[jnp.clip(inv[0, r * NB + c], 0, SLOTS)]
            return carry

        lax.fori_loop(lo, hi, one, 0)

    to_smem.wait()
    for c in loads[4:]:
        c.wait()
    build(0, NB)

    def hand_over(h):
        for i in (5, 6, 4, 3, 1, 2, 0):
            dy, dx = row_moves[i]
            feats[h][i].wait_recv()
            sib[h].append(put(h, rid(y - dy, swap(xh, dx), core), to_sib))

    hand_over(0)
    for c in sib[0]:
        c.wait_recv()

    own_rows = pl.ds(pl.multiple_of(xl * BLK, BLK), BLK)
    far_rows = pl.ds(pl.multiple_of((1 - xl) * BLK, BLK), BLK)
    moves = [4, 3, -3, 1, -1, 2, -2, 0]
    to_z = {k: (row, zmod(z + k) * 2 + xl) for k in (1, -1, 2, -2)}
    x_copy = {}
    near = {}

    def forward(i, h):
        t = zmod(z + moves[i])
        part[i, h] = jnp.dot(
            dense[pl.ds(pl.multiple_of(t * 2 * BLK, 2 * BLK), 2 * BLK), :], xall[h], preferred_element_type=F32
        )

    def cross(i, h):
        quant(part[i, h, far_rows, :], xs.at[h, i])
        x_copy[i, h] = push(xs.at[h, i], xr.at[h, i], to_xl)

    def joined(i, h):
        x_copy[i, h].wait_recv()
        return part[i, h, own_rows, :] + dequant(xr.at[h, i])

    def pass_on(v, src, dst, dev):
        quant(v, src)
        return push(src, dst, dev)

    def closer(i, h):
        near[i - 3, h] = pass_on(part[i, h], ns.at[h, i - 3], nr.at[h, i - 3], to_z[moves[i]])

    four = {}
    three = {}

    def outer(h):
        four[h] = pass_on(joined(0, h), fs.at[h], fr.at[h], to_z[2 - 4 * h])
        for k in range(2):
            three[k, h] = pass_on(joined(1 + k, h), ms.at[h, k], mr.at[h, k], to_z[1 - 2 * k])

    for i in (0, 1, 2, 5, 6):
        forward(i, 0)
        cross(i, 0)
    hand_over(1)
    for i in (3, 4):
        forward(i, 0)
        closer(i, 0)
    for c in sib[1]:
        c.wait_recv()
    for i in (0, 1, 2):
        forward(i, 1)
        cross(i, 1)
    outer(0)
    for i in (5, 6):
        forward(i, 1)
        cross(i, 1)
    forward(7, 0)
    for i in (3, 4):
        forward(i, 1)
        closer(i, 1)
    outer(1)
    forward(7, 1)
    for h in range(2):
        for k in range(2):
            near[k, h].wait_recv()
        part[7, h] = part[7, h] + dequant(nr.at[h, 0]) + dequant(nr.at[h, 1])
        cross(7, h)
    last = {}
    for h in range(2):
        for k in range(2):
            v = joined(5 + k, h)
            three[k, h].wait_recv()
            v = v + dequant(mr.at[h, k])
            if h == k:
                four[h].wait_recv()
                v = v + dequant(fr.at[h])
            last[k, h] = pass_on(v, es.at[h, k], er.at[h, k], to_z[2 - 4 * k])
    total = []
    for h in range(2):
        v = joined(7, h)
        for k in range(2):
            last[k, h].wait_recv()
            v = v + dequant(er.at[h, k])
        total.append(v)
    agg = jnp.concatenate(total, axis=1)

    w = weight[...]
    three = jnp.dot(split3(agg), w, preferred_element_type=F32)
    v = three[0:BLK] + three[BLK : 2 * BLK] + three[2 * BLK : 3 * BLK]
    v2 = v * v
    th = jnp.tanh(ROOT * (v + 0.044715 * (v2 * v)))
    act[...] = (0.5 * v * (1.0 + th)).astype(BF16)
    slope = 0.5 * (1.0 + th) + (0.5 * ROOT) * v * (1.0 - th * th) * (1.0 + 3 * 0.044715 * v2)
    grad_pre = cot[...].astype(F32) * slope
    tri = lax.dot_general(w, split3(grad_pre), (((1,), (1,)), ((), ())), preferred_element_type=F32)
    gt[col] = (tri[:, 0:BLK] + tri[:, BLK : 2 * BLK] + tri[:, 2 * BLK : 3 * BLK]).astype(BF16)

    far = 1 - xl

    def send(zz, lane, h, dev):
        spot = gt.at[zmod(zz) * 2 + lane, half[h]]
        return push(spot, spot, dev)

    g = {}
    for h in range(2):
        for k in (2, -2):
            g[k, h] = send(z, xl, h, to_z[k])
        g[0, h] = send(z, xl, h, to_xl)
        for k in (1, -1):
            g[k, h] = send(z, xl, h, to_z[k])

    def product(zz, n, h):
        t = zmod(zz)
        lhs = jnp.concatenate([gt[t * 2, half[h], :], gt[t * 2 + 1, half[h], :]], axis=1)
        rhs = dense[pl.ds(pl.multiple_of(t * 2 * BLK, 2 * BLK), 2 * BLK), pl.ds(pl.multiple_of(n * 2 * BLK, 2 * BLK), 2 * BLK)]
        return jnp.dot(lhs, rhs, preferred_element_type=F32)

    def add_to(zs_, n, h, fresh):
        total = product(zs_[0], n, h)
        for zz in zs_[1:]:
            total = total + product(zz, n, h)
        for k in range(2):
            old = 0.0 if fresh else qsum[2 * n + k, half[h], :]
            qsum[2 * n + k, half[h], :] = old + total[:, half[k]]

    def add_pass(zs_, h, fresh):
        for n in range(NB // 2):
            add_to(zs_, n, h, fresh)

    relay = {}
    beside = {}
    onto = {}
    for h in range(2):
        for k in (2, -2):
            one = k // 2
            g[k, h].wait_recv()
            relay[3 * one, h] = send(z - k, xl, h, to_z[one])
            if h == (1 - one) // 2:
                relay[4, h] = send(z - k, xl, h, to_z[k])
            onto[k, h] = send(z - k, xl, h, to_xl)
        g[0, h].wait_recv()
        for k in (1, -1):
            beside[k, h] = send(z, far, h, to_z[k])
    for h in range(2):
        add_pass([z], h, True)
        for k in (3, -3, 4):
            relay[k, h].wait_recv()
            onto[k, h] = send(z - k, xl, h, to_xl)
    for h in range(2):
        for k in (1, -1):
            g[k, h].wait_recv()
            beside[k, h].wait_recv()
        for k in (2, -2):
            onto[k, h].wait_recv()
        add_pass([z - 1, z + 1, z - 2, z + 2], h, False)

    order = row_moves + [(0, 0)]
    from_sib = {}
    sums = {}
    total = []

    def settle(i, h):
        dy, dx = order[i]
        n = rid(y + dy, swap(xh, dx), 0) // 2
        from_sib[i, h].wait_recv()
        value = qsum[2 * n + core, half[h], :] + sibr[i, half[h], :]
        if i < 7:
            sums[i, h] = pass_on(value, ds.at[h, i], dr.at[h, i], row_devs[i])
        return value

    for h in range(2):
        for k in (3, -3, 4):
            onto[k, h].wait_recv()
        for i, (dy, dx) in enumerate(order):
            n = rid(y + dy, swap(xh, dx), 0) // 2
            add_to([z + 3, z - 3, z + 4], n, h, False)
            from_sib[i, h] = push(qsum.at[2 * n + 1 - core, half[h]], sibr.at[i, half[h]], to_sib)
        for i in range(7):
            settle(i, h)
        total.append(settle(7, h))
    for h in range(2):
        for i in (5, 6, 4, 3, 1, 2, 0):
            sums[i, h].wait_recv()
            total[h] = total[h] + dequant(dr.at[h, i])
        gfeat[0, :, half[h]] = total[h].T

    for c in copies:
        c.wait_send()


def hand_out(act_in, grad_in, act, grad):
    act[...] = act_in[...]
    grad[...] = grad_in[...]


def body(features, weight, cotangent, block_vals, block_slots, block_count):
    vm = pl.BlockSpec(memory_space=pltpu.VMEM)
    hbm = pl.BlockSpec(memory_space=pltpu.HBM)
    v = pltpu.VMEM
    coded = (F + 16, BLK)
    small = (BLK + 16, BLK)
    i16 = jnp.int16
    shapes = (jax.ShapeDtypeStruct((BLK, F), BF16), jax.ShapeDtypeStruct((1, BLK, F), F32))
    results = pl.pallas_call(
        kernel,
        out_shape=shapes,
        in_specs=[hbm] * 6,
        out_specs=(vm, vm),
        scratch_shapes=[
            v((F, F), BF16),
            v((BLK, F), BF16),
            v((1, SLOTS), jnp.int32),
            v((1, 1), jnp.int32),
            v((8, NB * NB), jnp.int32),
            pltpu.SMEM((8, NB * NB), jnp.int32),
            v((SLOTS + 1, BLK, BLK), BF16),
            v((NB * BLK, NB * BLK), BF16),
            v((2, NB * BLK, BLK), BF16),
            v((8, 2, 2 * BLK, BLK), F32),
            v((NB, F, BLK), BF16),
            v((NB, F, BLK), F32),
            v((2, 8, *small), i16),
            v((2, 8, *small), i16),
            v((2, 2, *coded), i16),
            v((2, 2, *coded), i16),
            v((2, *small), i16),
            v((2, *small), i16),
            v((2, 2, *small), i16),
            v((2, 2, *small), i16),
            v((2, 2, *small), i16),
            v((2, 2, *small), i16),
            v((8, F, BLK), F32),
            v((2, 7, *small), i16),
            v((2, 7, *small), i16),
            pltpu.SemaphoreType.DMA((N_COPIES,)),
            pltpu.SemaphoreType.DMA((N_COPIES,)),
            pltpu.SemaphoreType.DMA((N_LOADS + 7,)),
        ],
        compiler_params=pltpu.CompilerParams(
            collective_id=0, has_side_effects=True, vmem_limit_bytes=56 * 1024 * 1024
        ),
        name="layer",
    )(features, weight, cotangent, block_vals.reshape(SLOTS, BLK, BLK), block_slots, block_count)
    return pl.pallas_call(
        hand_out,
        out_shape=shapes,
        in_specs=[vm] * 2,
        out_specs=(vm, vm),
        name="hand_out",
    )(*results)


def solution(mesh):
    return jax.shard_map(
        body,
        mesh=mesh,
        in_specs=(
            P("col", "row", None),
            P(),
            P(("row", "col"), None),
            P("row", "col", None, None, None),
            P("row", "col", None),
            P("row", "col"),
        ),
        out_specs=(P(("row", "col"), None), P("col", "row", None)),
        check_vma=False,
    )
```
